32 devices in a mesh: seq: 8 (over z, x), head: 4 (over y, core).
Axes of the slice: x: 2, y: 2, z: 4, core: 2. Of those that a mesh axis runs over, the one named last changes fastest.
Arguments:
- queries: bfloat16 [16, 4096, 128], P(None, ('seq', 'head')), may hold values from -0.5390625 to 0.5390625
- keys: bfloat16 [16, 4096, 128], P(None, ('seq', 'head')), may hold values from -0.5390625 to 0.5390625
- values: bfloat16 [16, 4096, 128], P(None, ('seq', 'head')), may hold values from -24 to 24
- out_grad: bfloat16 [16, 4096, 128], P(None, ('seq', 'head')), may hold values from -6 to 6
- regular: float32 [16, 128], P('head'), may hold values from 0.25 to 4
Outputs:
- output: bfloat16 [16, 4096, 128], P(None, ('seq', 'head'))
- query_grad: bfloat16 [16, 4096, 128], P(None, ('seq', 'head'))
- key_grad: bfloat16 [16, 4096, 128], P(None, ('seq', 'head'))
- value_grad: bfloat16 [16, 4096, 128], P(None, ('seq', 'head'))
The draws below stay inside these ranges and needn't reach their ends.
All inputs are finite; a program needn't handle non-finite values.
Results may differ from the reference program's by a relative error of at most 0.001.
Values may be sent and summed in bfloat16 or wider, within the bound.
A program may use at most 64 MiB of HBM per device.

```python
import math
from functools import partial
import jax
import jax.numpy as jnp
from jax import lax

HEADS = 16
DH = 128
GROUP = 128
TOKENS = 4096


def levels(key, shape, split, smallest, high):
    def one(dim, parts):
        heights = jax.random.uniform(jax.random.fold_in(jax.random.fold_in(key, 6), dim), (parts,), jnp.float32, smallest / len(split), high / len(split))
        return jnp.repeat(jnp.exp(heights), shape[dim] // parts).reshape((-1,) + (1,) * (len(shape) - dim - 1))

    factor_of = one(*split[0])
    for cut in split[1:]:
        factor_of = factor_of * one(*cut)
    return factor_of


def bell_draw(own_key, dims, spread, bound, shards=(), kind=jnp.bfloat16):
    level = levels(own_key, dims, shards, -0.22, 0.18) if shards else 1.0
    values = jax.random.normal(own_key, dims, jnp.float32) * spread * level
    return jnp.minimum(jnp.maximum(values, -bound), bound).astype(kind)


def setup_inputs(seed: int = 0) -> dict:
    key_list = jax.random.split(jax.random.key(seed), 6)
    return {
        "queries": bell_draw(key_list[0], (HEADS, TOKENS, DH), 0.09, 0.5390625, ((1, 32),)),
        "keys": bell_draw(key_list[1], (HEADS, TOKENS, DH), 0.09, 0.5390625, ((1, 32),)),
        "values": bell_draw(key_list[2], (HEADS, TOKENS, DH), 4.0, 24.0, ((1, 32),)),
        "out_grad": bell_draw(key_list[3], (HEADS, TOKENS, DH), 1.0, 6.0, ((1, 32),)),
        "regular": jnp.clip(jnp.exp(math.log(4.0) - 2.7725887 * jax.random.uniform(key_list[4], (HEADS, DH), jnp.float32) ** levels(key_list[4], (HEADS, DH), ((0, 4),), -0.2, 0.2)), 0.25, 4.0),
    }


def exact_einsum(form, left, right):
    return jnp.einsum(form, left, right, precision=lax.Precision.HIGHEST)

def group_output(query_rows, key_rows, value_rows, gram_in, state_in, causal):
    eye_dim = jnp.broadcast_to(jnp.eye(gram_in.shape[-1], dtype=jnp.float32), gram_in.shape)
    low_gram = jnp.linalg.cholesky(gram_in)
    half_inv = lax.linalg.triangular_solve(low_gram, eye_dim, left_side=True, lower=True)
    inverse = lax.linalg.triangular_solve(low_gram, half_inv, left_side=True, lower=True, transpose_a=True)
    key_inv = exact_einsum('...cd,...de->...ce', key_rows, inverse)
    inner_mat = exact_einsum('...ce,...te->...ct', key_inv, key_rows)
    eye_rows = jnp.eye(causal.shape[0], dtype=jnp.float32)
    low_mix = jnp.linalg.cholesky(inner_mat + eye_rows)
    right_side = exact_einsum('...ce,...te->...ct', key_inv, query_rows)
    first_pass = lax.linalg.triangular_solve(low_mix, right_side, left_side=True, lower=True) * causal
    second_pass = lax.linalg.triangular_solve(low_mix, first_pass, left_side=True, lower=True, transpose_a=True) * causal
    solved = exact_einsum('...de,...te->...dt', inverse, query_rows) - exact_einsum('...cd,...ct->...dt', key_inv, second_pass)
    scores = exact_einsum('...cd,...dt->...ct', key_rows, solved) * causal
    return exact_einsum('...ed,...dt->...te', state_in, solved) + exact_einsum('...ce,...ct->...te', value_rows, scores)

def reference(queries, keys, values, out_grad, regular):
    block_count = TOKENS // GROUP
    positions = jnp.arange(GROUP)
    causal = (positions[:, None] <= positions[None, :]).astype(jnp.float32)

    def blocks(array):
        return array.astype(jnp.float32).reshape(HEADS, block_count, GROUP, DH).transpose(1, 0, 2, 3)
    query_all, key_all, value_all, grad_all = (blocks(queries), blocks(keys), blocks(values), blocks(out_grad))
    base = regular.astype(jnp.float32)[:, :, None] * jnp.eye(DH, dtype=jnp.float32)
    zero_state = jnp.zeros((HEADS, DH, DH), jnp.float32)

    def forward(carried, inputs_now):
        gram_sum, state_sum = carried
        query_rows, key_rows, value_rows, grad_rows = inputs_now
        result, pull = jax.vjp(partial(group_output, causal=causal), query_rows, key_rows, value_rows, base + gram_sum, state_sum)
        grads = pull(grad_rows)
        gram_next = gram_sum + exact_einsum('hcd,hce->hde', key_rows, key_rows)
        state_next = state_sum + exact_einsum('hce,hcd->hed', value_rows, key_rows)
        return ((gram_next, state_next), (result,) + tuple(grads))
    unused, (result, dq_part, dk_part, dv_part, dgram_part, dstate_part) = lax.scan(forward, (zero_state, zero_state), (query_all, key_all, value_all, grad_all))

    def backward(carried, inputs_now):
        gram_after, state_after = carried
        key_rows, value_rows, dk_rows, dv_rows, dgram_rows, dstate_rows = inputs_now
        sym_after = gram_after + jnp.swapaxes(gram_after, -1, -2)
        dk_full = dk_rows + exact_einsum('hde,hce->hcd', sym_after, key_rows) + exact_einsum('hed,hce->hcd', state_after, value_rows)
        dv_full = dv_rows + exact_einsum('hed,hcd->hce', state_after, key_rows)
        return ((gram_after + dgram_rows, state_after + dstate_rows), (dk_full, dv_full))
    unused_back, (dk_total, dv_total) = lax.scan(backward, (zero_state, zero_state), (key_all, value_all, dk_part, dv_part, dgram_part, dstate_part), reverse=True)

    def unblock(array):
        return array.transpose(1, 0, 2, 3).reshape(HEADS, TOKENS, DH).astype(jnp.bfloat16)
    return (unblock(result), unblock(dq_part), unblock(dk_total), unblock(dv_total))
```

```python
import functools

import jax
import jax.numpy as jnp
from jax import lax
from jax.experimental import pallas as pl
from jax.experimental.pallas import tpu as pltpu
from jax.sharding import PartitionSpec as P

GROUP = 128
BASE = 32
VMEM_LIMIT = 56 * 1024 * 1024
F32 = jnp.float32
BF16 = jnp.bfloat16
DIMS = {
    "nn": (((1,), (0,)), ((), ())),
    "nt": (((1,), (1,)), ((), ())),
    "tn": (((0,), (0,)), ((), ())),
}


def parts(x, count):
    if isinstance(x, list):
        return x[:count]
    if x.dtype == BF16:
        return [x]
    found = []
    for i in range(count):
        term = x.astype(BF16)
        found.append(term)
        if i + 1 < count:
            x = x - term.astype(F32)
    return found


def mm(a, b, form="nn", count=2):
    left, right = parts(a, count), parts(b, count)
    total = None
    for i in reversed(range(len(left))):
        for j in reversed(range(len(right))):
            if i + j < count:
                term = lax.dot_general(left[i], right[j], DIMS[form], preferred_element_type=F32)
                total = term if total is None else total + term
    return total


def iota(shape, dim):
    return lax.broadcasted_iota(jnp.int32, shape, dim)


def take_block(ref, per_block, heads, head, block):
    rows = [ref[(block * per_block + r) * heads + head] for r in range(per_block)]
    return rows[0] if per_block == 1 else jnp.concatenate(rows, axis=0)


def put_block(ref, per_block, heads, head, block, value):
    size = value.shape[0] // per_block
    for r in range(per_block):
        ref[(block * per_block + r) * heads + head] = value[r * size : (r + 1) * size]


def eliminate(x, groups):
    shape = (groups, BASE, 128)
    flat = (groups * BASE, 128)
    lane = iota(shape, 2) % BASE
    row = iota(shape, 1)
    group_start = (iota(flat, 1) // BASE) * BASE
    x = x.reshape(shape)
    pivots = jnp.ones(shape, F32)
    for p in range(BASE):
        column = jnp.take_along_axis(
            x.reshape(flat), group_start + p, axis=1, mode="promise_in_bounds"
        ).reshape(shape)
        pivot = column[:, p : p + 1, :]
        pivots = jnp.where(row == p, pivot, pivots)
        if p + 1 < BASE:
            pivot_row = jnp.where(lane[:, p : p + 1] == p, 1.0, x[:, p : p + 1, :])
            scaled = pivot_row * (1.0 / pivot)
            keep = jnp.where(lane == p, 0.0, x)
            x = jnp.where(row > p, keep - column * scaled, x)
    unit = jnp.where(lane < row, x, jnp.where(lane == row, 1.0, 0.0))
    return (unit * lax.rsqrt(pivots)).reshape(flat)


def factor(a_ref, packed_ref, pairs, invert):
    groups = pairs // 4
    slab = (BASE, 128)
    square = (128, 128)

    def one_block(kb, carry):
        start = pl.multiple_of(kb * BASE, BASE)
        slab_group = iota(slab, 1) // BASE
        slabs = []
        for g in range(groups):
            joined = jnp.zeros(slab, F32)
            for h in range(4):
                rows = a_ref[4 * g + h, pl.ds(start, BASE), :]
                rows = pltpu.roll(rows, lax.rem((h - kb) * BASE + 128, 128), 1)
                joined = jnp.where(slab_group == h, rows, joined)
            slabs.append(joined)
        packed_ref[...] = eliminate(jnp.concatenate(slabs, axis=0), groups)

        def update(g, carry):
            packed = packed_ref[pl.ds(pl.multiple_of(g * BASE, BASE), BASE), :]
            row_block = iota(square, 0) // BASE
            col_block = iota(square, 1) // BASE
            eye = (iota(square, 0) == iota(square, 1)).astype(F32)
            for h in range(4):
                pair = 4 * g + h
                turned = pltpu.roll(packed, lax.rem((kb - h) * BASE + 128, 128), 1)
                low = parts(jnp.where(slab_group == kb, turned, 0.0), 3)
                a = a_ref[pair]
                with_eye = jnp.where((row_block == kb) & (col_block == kb), eye, a)
                top = mm(low, with_eye, "nn", 3)
                wide = mm(low, top, "tn", 3)
                new = jnp.where(col_block == kb, 0.0, a) - mm(a, wide, "nn", 3)
                if invert:
                    a_ref[pair] = jnp.where(row_block == kb, wide, new)
                else:
                    a_ref[pair] = jnp.where(row_block > kb, new, a)
                    a_ref[pair, pl.ds(start, BASE), :] = jnp.where(slab_group <= kb, top, 0.0)
            return carry

        lax.fori_loop(0, groups, update, 0)
        return carry

    lax.fori_loop(0, 128 // BASE, one_block, 0)


def sums_kernel(heads, blocks, per_block, k_ref, v_ref, out_ref):
    def one(head, carry):
        gram = jnp.zeros((128, 128), F32)
        state = jnp.zeros((128, 128), F32)
        for block in range(blocks):
            k = take_block(k_ref, per_block, heads, head, block)
            v = take_block(v_ref, per_block, heads, head, block)
            gram += mm(k, k, "tn")
            state += mm(v, k, "tn")
        out_ref[head] = gram
        out_ref[heads + head] = state
        return carry

    lax.fori_loop(0, heads, one, 0)


def main_kernel(
    heads, blocks, per_block,
    q_ref, k_ref, v_ref, g_ref, every_ref, regular_ref,
    o_ref, dq_ref, dk_ref, dv_ref, later_ref, sums_ref,
    p_ref, kp_ref, m_ref, state_ref, packed_ref,
):
    pairs = heads * blocks
    square = (128, 128)
    rank = lax.axis_index("seq")

    def prefix(head, carry):
        def add(s, so_far):
            return (so_far[0] + every_ref[s, head], so_far[1] + every_ref[s, heads + head])

        zero = jnp.zeros(square, F32)
        gram, state = lax.fori_loop(0, rank, add, (zero, zero))
        eye = iota(square, 0) == iota(square, 1)
        gram = gram + jnp.where(eye, regular_ref[pl.ds(head, 1), :], 0.0)
        for block in range(blocks):
            p_ref[head * blocks + block] = gram
            state_ref[head * blocks + block] = state
            if block + 1 < blocks:
                k = take_block(k_ref, per_block, heads, head, block)
                v = take_block(v_ref, per_block, heads, head, block)
                gram += mm(k, k, "tn")
                state += mm(v, k, "tn")
        return carry

    lax.fori_loop(0, heads, prefix, 0)
    factor(p_ref, packed_ref, pairs, True)

    def inner(head, carry):
        eye = (iota(square, 0) == iota(square, 1)).astype(F32)
        for block in range(blocks):
            pair = head * blocks + block
            k = take_block(k_ref, per_block, heads, head, block)
            kp = mm(k, p_ref[pair], "nn", 3)
            kp_ref[pair] = kp
            m_ref[pair] = eye + mm(kp, k, "nt", 3)
        return carry

    lax.fori_loop(0, heads, inner, 0)
    factor(m_ref, packed_ref, pairs, False)

    def outer(head, carry):
        upto = iota(square, 1) <= iota(square, 0)
        later_gram = jnp.zeros(square, F32)
        later_state = jnp.zeros(square, F32)
        for block in reversed(range(blocks)):
            pair = head * blocks + block
            q = take_block(q_ref, per_block, heads, head, block)
            k = take_block(k_ref, per_block, heads, head, block)
            v = take_block(v_ref, per_block, heads, head, block)
            g = take_block(g_ref, per_block, heads, head, block)
            inverse = parts(p_ref[pair], 3)
            kp = parts(kp_ref[pair], 3)
            m = parts(m_ref[pair], 3)
            state = parts(state_ref[pair], 2)

            def solve(rows):
                rows = parts(rows, 3)
                y = jnp.where(upto, mm(mm(rows, kp, "nt", 3), m, "nt", 3), 0.0)
                x = jnp.where(upto, mm(y, m, "nn", 3), 0.0)
                return mm(rows, inverse, "nn", 3) - mm(x, kp, "nn", 3)

            u = solve(q)
            ct = jnp.where(upto, mm(g, v, "nt"), 0.0)
            z = solve(mm(g, state, "nn") + mm(ct, k, "nn"))
            up, zp = parts(u, 2), parts(z, 2)
            wt = parts(jnp.where(upto, mm(up, k, "nt"), 0.0), 2)
            w2t = jnp.where(upto, mm(zp, k, "nt"), 0.0)
            put_block(o_ref, per_block, heads, head, block, (mm(up, state, "nt") + mm(wt, v, "nn")).astype(BF16))
            put_block(dq_ref, per_block, heads, head, block, z.astype(BF16))
            dk_ref[pair] = mm(ct - w2t, up, "tn") - mm(wt, zp, "tn")
            dv_ref[pair] = mm(wt, g, "tn")
            later_ref[pair] = later_gram
            later_ref[pairs + pair] = later_state
            zu = mm(zp, up, "tn")
            later_gram = later_gram - (zu + zu.T)
            later_state = later_state + mm(g, up, "tn")
        sums_ref[head] = later_gram
        sums_ref[heads + head] = later_state
        return carry

    lax.fori_loop(0, heads, outer, 0)


def last_kernel(
    heads, blocks, per_block, shards,
    k_ref, v_ref, dk_ref, dv_ref, later_ref, every_ref, dk_out, dv_out,
):
    pairs = heads * blocks
    rank = lax.axis_index("seq")

    def one(head, carry):
        def add(s, so_far):
            return (so_far[0] + every_ref[s, head], so_far[1] + every_ref[s, heads + head])

        zero = jnp.zeros((128, 128), F32)
        gram, state = lax.fori_loop(rank + 1, shards, add, (zero, zero))
        for block in range(blocks):
            pair = head * blocks + block
            k = take_block(k_ref, per_block, heads, head, block)
            v = take_block(v_ref, per_block, heads, head, block)
            sym = later_ref[pair] + gram
            after = parts(later_ref[pairs + pair] + state, 2)
            dk = dk_ref[pair] + mm(k, sym, "nn") + mm(v, after, "nn")
            dv = dv_ref[pair] + mm(k, after, "nt")
            put_block(dk_out, per_block, heads, head, block, dk.astype(BF16))
            put_block(dv_out, per_block, heads, head, block, dv.astype(BF16))
        return carry

    lax.fori_loop(0, heads, one, 0)


def call(body, inputs, out_shape, scratch=(), flops=10**9):
    vmem = pl.BlockSpec(memory_space=pltpu.VMEM)
    return pl.pallas_call(
        body,
        out_shape=out_shape,
        in_specs=[vmem] * len(inputs),
        out_specs=jax.tree.map(lambda _: vmem, out_shape),
        scratch_shapes=list(scratch),
        compiler_params=pltpu.CompilerParams(vmem_limit_bytes=VMEM_LIMIT),
        cost_estimate=pl.CostEstimate(flops=flops, bytes_accessed=8 * 2**20, transcendentals=0),
    )(*inputs)


def on_device(head_parts, seq_parts, queries, keys, values, out_grad, regular):
    local = queries.shape[1]
    feature = queries.shape[2]
    heads = queries.shape[0] // head_parts
    blocks = head_parts * local // GROUP
    per_block = GROUP // local
    pairs = heads * blocks

    def swap(x):
        return lax.all_to_all(x, "head", split_axis=0, concat_axis=0, tiled=True)

    keys, values = swap(keys), swap(values)
    queries, out_grad = swap(queries), swap(out_grad)
    square = (feature, feature)

    def shape(count, kind=F32, rows=feature):
        return jax.ShapeDtypeStruct((count, rows, feature), kind)

    moved = jax.ShapeDtypeStruct(queries.shape, BF16)
    sums = call(functools.partial(sums_kernel, heads, blocks, per_block), (keys, values), shape(2 * heads))
    every = lax.all_gather(sums, "seq", axis=0)
    output, dq, dk, dv, later, back = call(
        functools.partial(main_kernel, heads, blocks, per_block),
        (queries, keys, values, out_grad, every, regular),
        (moved, moved, shape(pairs), shape(pairs), shape(2 * pairs), shape(2 * heads)),
        [pltpu.VMEM((pairs,) + square, F32)] * 4 + [pltpu.VMEM((pairs // 4 * BASE, 128), F32)],
    )
    every_back = lax.all_gather(back, "seq", axis=0)
    output, dq = swap(output), swap(dq)
    dk, dv = call(
        functools.partial(last_kernel, heads, blocks, per_block, seq_parts),
        (keys, values, dk, dv, later, every_back),
        (moved, moved),
    )
    return output, dq, swap(dk), swap(dv)


def solution(mesh):
    placed = P(None, ("seq", "head"), None)
    return jax.shard_map(
        functools.partial(on_device, mesh.shape["head"], mesh.shape["seq"]),
        mesh=mesh,
        in_specs=(placed,) * 4 + (P("head", None),),
        out_specs=(placed,) * 4,
        check_vma=False,
    )
```

```python
import functools

import jax
import jax.numpy as jnp
from jax import lax
from jax.experimental import pallas as pl
from jax.experimental.pallas import tpu as pltpu
from jax.sharding import PartitionSpec as P

GROUP = 128
BASE = 32
VMEM_LIMIT = 56 * 1024 * 1024
F32 = jnp.float32
BF16 = jnp.bfloat16
DIMS = {
    "nn": (((1,), (0,)), ((), ())),
    "nt": (((1,), (1,)), ((), ())),
    "tn": (((0,), (0,)), ((), ())),
}


def parts(x, count):
    if isinstance(x, list):
        return x[:count]
    if x.dtype == BF16:
        return [x]
    found = []
    for i in range(count):
        term = x.astype(BF16)
        found.append(term)
        if i + 1 < count:
            x = x - term.astype(F32)
    return found


def mm(a, b, form="nn", count=2):
    left, right = parts(a, count), parts(b, count)
    total = None
    for i in reversed(range(len(left))):
        for j in reversed(range(len(right))):
            if i + j < count:
                term = lax.dot_general(left[i], right[j], DIMS[form], preferred_element_type=F32)
                total = term if total is None else total + term
    return total


def iota(shape, dim):
    return lax.broadcasted_iota(jnp.int32, shape, dim)


def take_block(ref, per_block, heads, head, block):
    rows = [ref[(block * per_block + r) * heads + head] for r in range(per_block)]
    return rows[0] if per_block == 1 else jnp.concatenate(rows, axis=0)


def put_block(ref, per_block, heads, head, block, value):
    size = value.shape[0] // per_block
    for r in range(per_block):
        ref[(block * per_block + r) * heads + head] = value[r * size : (r + 1) * size]


def eliminate(x, groups):
    shape = (groups, BASE, 128)
    flat = (groups * BASE, 128)
    lane = iota(shape, 2) % BASE
    row = iota(shape, 1)
    group_start = (iota(flat, 1) // BASE) * BASE
    x = x.reshape(shape)
    pivots = jnp.ones(shape, F32)
    for p in range(BASE):
        column = jnp.take_along_axis(
            x.reshape(flat), group_start + p, axis=1, mode="promise_in_bounds"
        ).reshape(shape)
        pivot = column[:, p : p + 1, :]
        pivots = jnp.where(row == p, pivot, pivots)
        if p + 1 < BASE:
            pivot_row = jnp.where(lane[:, p : p + 1] == p, 1.0, x[:, p : p + 1, :])
            scaled = pivot_row * (1.0 / pivot)
            keep = jnp.where(lane == p, 0.0, x)
            x = jnp.where(row > p, keep - column * scaled, x)
    unit = jnp.where(lane < row, x, jnp.where(lane == row, 1.0, 0.0))
    return (unit * lax.rsqrt(pivots)).reshape(flat)


def factor(a_ref, packed_ref, pairs, invert):
    groups = pairs // 4
    slab = (BASE, 128)
    square = (128, 128)

    def one_block(kb, carry):
        start = pl.multiple_of(kb * BASE, BASE)
        slab_group = iota(slab, 1) // BASE
        slabs = []
        for g in range(groups):
            joined = jnp.zeros(slab, F32)
            for h in range(4):
                rows = a_ref[4 * g + h, pl.ds(start, BASE), :]
                rows = pltpu.roll(rows, lax.rem((h - kb) * BASE + 128, 128), 1)
                joined = jnp.where(slab_group == h, rows, joined)
            slabs.append(joined)
        packed_ref[...] = eliminate(jnp.concatenate(slabs, axis=0), groups)

        def update(g, carry):
            packed = packed_ref[pl.ds(pl.multiple_of(g * BASE, BASE), BASE), :]
            row_block = iota(square, 0) // BASE
            col_block = iota(square, 1) // BASE
            eye = (iota(square, 0) == iota(square, 1)).astype(F32)
            for h in range(4):
                pair = 4 * g + h
                turned = pltpu.roll(packed, lax.rem((kb - h) * BASE + 128, 128), 1)
                low = parts(jnp.where(slab_group == kb, turned, 0.0), 3)
                a = a_ref[pair]
                with_eye = jnp.where((row_block == kb) & (col_block == kb), eye, a)
                top = mm(low, with_eye, "nn", 3)
                wide = mm(low, top, "tn", 3)
                new = jnp.where(col_block == kb, 0.0, a) - mm(a, wide, "nn", 3)
                if invert:
                    a_ref[pair] = jnp.where(row_block == kb, wide, new)
                else:
                    a_ref[pair] = jnp.where(row_block > kb, new, a)
                    a_ref[pair, pl.ds(start, BASE), :] = jnp.where(slab_group <= kb, top, 0.0)
            return carry

        lax.fori_loop(0, groups, update, 0)
        return carry

    lax.fori_loop(0, 128 // BASE, one_block, 0)


def group_size(shards):
    size = 1
    while 4 * size * size <= shards and shards % (2 * size) == 0:
        size *= 2
    return size


def send(src, dst, send_sem, recv_sem, where):
    return pltpu.make_async_remote_copy(
        src_ref=src, dst_ref=dst, send_sem=send_sem, recv_sem=recv_sem,
        device_id=where, device_id_type=pl.DeviceIdType.MESH,
    )


def meet(head_parts, shards):
    size = group_size(shards)
    rank, me = lax.axis_index("seq"), lax.axis_index("head")
    outer, inner = rank // size, rank % size
    barrier = pltpu.get_barrier_semaphore()

    def greet(where):
        pl.semaphore_signal(barrier, inc=1, device_id=where, device_id_type=pl.DeviceIdType.MESH)

    for d in range(1, head_parts):
        greet((rank, lax.rem(me + d, head_parts)))
    for d in range(1, size):
        greet((outer * size + lax.rem(inner + d, size), me))

    @pl.when(outer > 0)
    def _():
        greet((rank - size, me))

    @pl.when(outer < shards // size - 1)
    def _():
        greet((rank + size, me))

    chained = jnp.where(outer > 0, 1, 0) + jnp.where(outer < shards // size - 1, 1, 0)
    pl.semaphore_wait(barrier, head_parts - 1 + size - 1 + chained)


class Scan:
    def __init__(self, shards, backward, own, near, before, total, sems):
        self.size = group_size(shards)
        self.count = shards // self.size
        self.rank, self.me = lax.axis_index("seq"), lax.axis_index("head")
        self.step = -self.size if backward else self.size
        self.base = self.rank // self.size * self.size
        self.inner = self.rank % self.size
        outer = self.rank // self.size
        self.outer = self.count - 1 - outer if backward else outer
        self.backward = backward
        self.own, self.near, self.before, self.total = own, near, before, total
        self.near_send, self.near_recv, self.far_send, self.far_recv = sems

    def near_copy(self, c, d):
        where = (self.base + lax.rem(self.inner + d, self.size), self.me)
        return send(
            self.own.at[c], self.near.at[d - 1, c],
            self.near_send.at[d - 1, c], self.near_recv.at[d - 1, c], where,
        )

    def far_copy(self, c):
        where = (self.rank + self.step, self.me)
        return send(self.total.at[c], self.before.at[c], self.far_send.at[c], self.far_recv.at[c], where)

    def start(self, c):
        for d in range(1, self.size):
            self.near_copy(c, d).start()

    def finish(self, c):
        whole = self.own[c]
        lower = jnp.zeros(whole.shape, F32)
        for d in range(1, self.size):
            self.near_copy(c, d).wait_recv()
            other = self.near[d - 1, c]
            whole = whole + other
            counts = d > self.inner if self.backward else d <= self.inner
            lower = lower + jnp.where(counts, other, 0.0)

        @pl.when(self.outer == 0)
        def _():
            self.before[c] = jnp.zeros(whole.shape, F32)

        @pl.when(self.outer > 0)
        def _():
            self.far_copy(c).wait_recv()

        before = self.before[c]

        @pl.when(self.outer < self.count - 1)
        def _():
            self.total[c] = before + whole
            self.far_copy(c).start()

        return before + lower

    def drain(self, c):
        for d in range(1, self.size):
            self.near_copy(c, d).wait_send()

        @pl.when(self.outer < self.count - 1)
        def _():
            self.far_copy(c).wait_send()


def scan_scratch(shards, heads, square):
    size = group_size(shards)
    count = 2 * heads
    near = (max(size - 1, 1), count)
    dma = pltpu.SemaphoreType.DMA
    return [
        pltpu.VMEM(near + square, F32), pltpu.VMEM((count,) + square, F32),
        pltpu.VMEM((count,) + square, F32), dma(near), dma(near), dma((count,)), dma((count,)),
    ]


def first_kernel(
    heads, blocks, per_block, head_parts, shards,
    q_in, k_in, v_in, g_in, q_ref, k_ref, v_ref, g_ref, before_ref,
    own, near, before, total, near_send, near_recv, far_send, far_recv,
    one_send, one_recv, all_send, all_recv,
):
    rank, me = lax.axis_index("seq"), lax.axis_index("head")
    meet(head_parts, shards)
    scan = Scan(shards, False, own, near, before, total, (near_send, near_recv, far_send, far_recv))

    def one_copy(i, d, h):
        src, dst = ((k_in, k_ref), (v_in, v_ref))[i]
        peer = lax.rem(me + d, head_parts)
        return send(
            src.at[peer * heads + h], dst.at[me * heads + h],
            one_send.at[i, d - 1, h], one_recv.at[i, d - 1, h], (rank, peer),
        )

    def all_copy(i, d):
        src, dst = ((q_in, q_ref), (g_in, g_ref))[i]
        peer = lax.rem(me + d, head_parts)
        return send(
            src.at[pl.ds(peer * heads, heads)], dst.at[pl.ds(me * heads, heads)],
            all_send.at[i, d - 1], all_recv.at[i, d - 1], (rank, peer),
        )

    steps = [(i, d, h) for h in range(heads) for i in range(2) for d in range(1, head_parts)]
    wholes = [(i, d) for i in range(2) for d in range(1, head_parts)]
    for step in steps:
        one_copy(*step).start()
    for step in wholes:
        all_copy(*step).start()
    for src, dst in ((k_in, k_ref), (v_in, v_ref), (q_in, q_ref), (g_in, g_ref)):
        for h in range(heads):
            dst[me * heads + h] = src[me * heads + h]
    for h in range(heads):
        for i in range(2):
            for d in range(1, head_parts):
                one_copy(i, d, h).wait_recv()
        gram = jnp.zeros((128, 128), F32)
        state = jnp.zeros((128, 128), F32)
        for block in range(blocks):
            k = take_block(k_ref, per_block, heads, h, block)
            v = take_block(v_ref, per_block, heads, h, block)
            gram += mm(k, k, "tn")
            state += mm(v, k, "tn")
        own[2 * h] = gram
        own[2 * h + 1] = state
        scan.start(2 * h)
        scan.start(2 * h + 1)
    for c in range(2 * heads):
        before_ref[c] = scan.finish(c)
    for step in wholes:
        all_copy(*step).wait_recv()
    for c in range(2 * heads):
        scan.drain(c)
    for step in steps:
        one_copy(*step).wait_send()
    for step in wholes:
        all_copy(*step).wait_send()


def main_kernel(
    heads, blocks, per_block,
    q_ref, k_ref, v_ref, g_ref, before_ref, regular_ref,
    o_ref, dq_ref, dk_ref, dv_ref, later_ref, sums_ref,
    p_ref, kp_ref, m_ref, state_ref, packed_ref,
):
    pairs = heads * blocks
    square = (128, 128)

    def prefix(head, carry):
        gram, state = before_ref[2 * head], before_ref[2 * head + 1]
        eye = iota(square, 0) == iota(square, 1)
        gram = gram + jnp.where(eye, regular_ref[pl.ds(head, 1), :], 0.0)
        for block in range(blocks):
            p_ref[head * blocks + block] = gram
            state_ref[head * blocks + block] = state
            if block + 1 < blocks:
                k = take_block(k_ref, per_block, heads, head, block)
                v = take_block(v_ref, per_block, heads, head, block)
                gram += mm(k, k, "tn")
                state += mm(v, k, "tn")
        return carry

    lax.fori_loop(0, heads, prefix, 0)
    factor(p_ref, packed_ref, pairs, True)

    def inner(head, carry):
        eye = (iota(square, 0) == iota(square, 1)).astype(F32)
        for block in range(blocks):
            pair = head * blocks + block
            k = take_block(k_ref, per_block, heads, head, block)
            kp = mm(k, p_ref[pair], "nn", 3)
            kp_ref[pair] = kp
            m_ref[pair] = eye + mm(kp, k, "nt", 3)
        return carry

    lax.fori_loop(0, heads, inner, 0)
    factor(m_ref, packed_ref, pairs, False)

    def outer(head, carry):
        upto = iota(square, 1) <= iota(square, 0)
        later_gram = jnp.zeros(square, F32)
        later_state = jnp.zeros(square, F32)
        for block in reversed(range(blocks)):
            pair = head * blocks + block
            q = take_block(q_ref, per_block, heads, head, block)
            k = take_block(k_ref, per_block, heads, head, block)
            v = take_block(v_ref, per_block, heads, head, block)
            g = take_block(g_ref, per_block, heads, head, block)
            inverse = parts(p_ref[pair], 3)
            kp = parts(kp_ref[pair], 3)
            m = parts(m_ref[pair], 3)
            state = parts(state_ref[pair], 2)

            def solve(rows):
                rows = parts(rows, 3)
                y = jnp.where(upto, mm(mm(rows, kp, "nt", 3), m, "nt", 3), 0.0)
                x = jnp.where(upto, mm(y, m, "nn", 3), 0.0)
                return mm(rows, inverse, "nn", 3) - mm(x, kp, "nn", 3)

            u = solve(q)
            ct = jnp.where(upto, mm(g, v, "nt"), 0.0)
            z = solve(mm(g, state, "nn") + mm(ct, k, "nn"))
            up, zp = parts(u, 2), parts(z, 2)
            wt = parts(jnp.where(upto, mm(up, k, "nt"), 0.0), 2)
            w2t = jnp.where(upto, mm(zp, k, "nt"), 0.0)
            put_block(o_ref, per_block, heads, head, block, (mm(up, state, "nt") + mm(wt, v, "nn")).astype(BF16))
            put_block(dq_ref, per_block, heads, head, block, z.astype(BF16))
            dk_ref[pair] = mm(ct - w2t, up, "tn") - mm(wt, zp, "tn")
            dv_ref[pair] = mm(wt, g, "tn")
            later_ref[pair] = later_gram
            later_ref[pairs + pair] = later_state
            zu = mm(zp, up, "tn")
            later_gram = later_gram - (zu + zu.T)
            later_state = later_state + mm(g, up, "tn")
        sums_ref[2 * head] = later_gram
        sums_ref[2 * head + 1] = later_state
        return carry

    lax.fori_loop(0, heads, outer, 0)


def last_kernel(
    heads, blocks, per_block, head_parts, shards,
    o_in, dq_in, k_ref, v_ref, dk_ref, dv_ref, later_ref, own, o_out, dq_out, dk_out, dv_out,
    dk_all, dv_all, near, after, total, near_send, near_recv, far_send, far_recv,
    one_send, one_recv, all_send, all_recv,
):
    pairs = heads * blocks
    rank, me = lax.axis_index("seq"), lax.axis_index("head")
    meet(head_parts, shards)
    scan = Scan(shards, True, own, near, after, total, (near_send, near_recv, far_send, far_recv))

    def one_copy(i, d, h):
        src, dst = ((dk_all, dk_out), (dv_all, dv_out))[i]
        peer = lax.rem(me + d, head_parts)
        return send(
            src.at[peer * heads + h], dst.at[me * heads + h],
            one_send.at[i, d - 1, h], one_recv.at[i, d - 1, h], (rank, peer),
        )

    def all_copy(i, d):
        src, dst = ((o_in, o_out), (dq_in, dq_out))[i]
        peer = lax.rem(me + d, head_parts)
        return send(
            src.at[pl.ds(peer * heads, heads)], dst.at[pl.ds(me * heads, heads)],
            all_send.at[i, d - 1], all_recv.at[i, d - 1], (rank, peer),
        )

    steps = [(i, d, h) for h in range(heads) for i in range(2) for d in range(1, head_parts)]
    wholes = [(i, d) for i in range(2) for d in range(1, head_parts)]
    for c in range(2 * heads):
        scan.start(c)
    for step in wholes:
        all_copy(*step).start()
    for src, dst in ((o_in, o_out), (dq_in, dq_out)):
        for h in range(heads):
            dst[me * heads + h] = src[me * heads + h]
    for h in range(heads):
        gram, state = scan.finish(2 * h), scan.finish(2 * h + 1)
        for block in range(blocks):
            pair = h * blocks + block
            k = take_block(k_ref, per_block, heads, h, block)
            v = take_block(v_ref, per_block, heads, h, block)
            sym = later_ref[pair] + gram
            state_after = parts(later_ref[pairs + pair] + state, 2)
            dk = dk_ref[pair] + mm(k, sym, "nn") + mm(v, state_after, "nn")
            dv = dv_ref[pair] + mm(k, state_after, "nt")
            put_block(dk_all, per_block, heads, h, block, dk.astype(BF16))
            put_block(dv_all, per_block, heads, h, block, dv.astype(BF16))
        for i in range(2):
            for d in range(1, head_parts):
                one_copy(i, d, h).start()
        dk_out[me * heads + h] = dk_all[me * heads + h]
        dv_out[me * heads + h] = dv_all[me * heads + h]
    for step in wholes:
        all_copy(*step).wait_recv()
    for step in steps:
        one_copy(*step).wait_recv()
    for c in range(2 * heads):
        scan.drain(c)
    for step in wholes:
        all_copy(*step).wait_send()
    for step in steps:
        one_copy(*step).wait_send()


def call(body, inputs, out_shape, scratch=(), flops=10**9, **params):
    vmem = pl.BlockSpec(memory_space=pltpu.VMEM)
    return pl.pallas_call(
        body,
        out_shape=out_shape,
        in_specs=[vmem] * len(inputs),
        out_specs=jax.tree.map(lambda _: vmem, out_shape),
        scratch_shapes=list(scratch),
        compiler_params=pltpu.CompilerParams(vmem_limit_bytes=VMEM_LIMIT, **params),
        cost_estimate=pl.CostEstimate(flops=flops, bytes_accessed=8 * 2**20, transcendentals=0),
    )(*inputs)


def on_device(head_parts, seq_parts, queries, keys, values, out_grad, regular):
    local = queries.shape[1]
    feature = queries.shape[2]
    heads = queries.shape[0] // head_parts
    blocks = head_parts * local // GROUP
    per_block = GROUP // local
    pairs = heads * blocks

    square = (feature, feature)

    def shape(count, kind=F32, rows=feature):
        return jax.ShapeDtypeStruct((count, rows, feature), kind)

    moved = jax.ShapeDtypeStruct(queries.shape, BF16)
    square_sums = shape(2 * heads)
    dma = pltpu.SemaphoreType.DMA
    away = max(head_parts - 1, 1)
    swap_sems = [dma((2, away, heads))] * 2 + [dma((2, away))] * 2
    sizes = (heads, blocks, per_block)
    queries, keys, values, out_grad, before = call(
        functools.partial(first_kernel, *sizes, head_parts, seq_parts),
        (queries, keys, values, out_grad),
        (moved,) * 4 + (square_sums,),
        [pltpu.VMEM((2 * heads,) + square, F32)] + scan_scratch(seq_parts, heads, square) + swap_sems,
        collective_id=0, has_side_effects=True,
    )
    output, dq, dk, dv, later, back = call(
        functools.partial(main_kernel, *sizes),
        (queries, keys, values, out_grad, before, regular),
        (moved, moved, shape(pairs), shape(pairs), shape(2 * pairs), square_sums),
        [pltpu.VMEM((pairs,) + square, F32)] * 4 + [pltpu.VMEM((pairs // 4 * BASE, 128), F32)],
    )
    return call(
        functools.partial(last_kernel, *sizes, head_parts, seq_parts),
        (output, dq, keys, values, dk, dv, later, back),
        (moved,) * 4,
        [pltpu.VMEM(moved.shape, BF16)] * 2 + scan_scratch(seq_parts, heads, square) + swap_sems,
        collective_id=1, has_side_effects=True,
    )


def solution(mesh):
    placed = P(None, ("seq", "head"), None)
    return jax.shard_map(
        functools.partial(on_device, mesh.shape["head"], mesh.shape["seq"]),
        mesh=mesh,
        in_specs=(placed,) * 4 + (P("head", None),),
        out_specs=(placed,) * 4,
        check_vma=False,
    )
```

```python
import functools

import jax
import jax.numpy as jnp
from jax import lax
from jax.experimental import pallas as pl
from jax.experimental.pallas import tpu as pltpu
from jax.sharding import PartitionSpec as P

GROUP = 128
BASE = 32
VMEM_LIMIT = 56 * 1024 * 1024
F32 = jnp.float32
BF16 = jnp.bfloat16
DIMS = {
    "nn": (((1,), (0,)), ((), ())),
    "nt": (((1,), (1,)), ((), ())),
    "tn": (((0,), (0,)), ((), ())),
}


def parts(x, count):
    if isinstance(x, list):
        return x[:count]
    if x.dtype == BF16:
        return [x]
    found = []
    for i in range(count):
        term = x.astype(BF16)
        found.append(term)
        if i + 1 < count:
            x = x - term.astype(F32)
    return found


def mm(a, b, form="nn", count=2):
    left, right = parts(a, count), parts(b, count)
    pairs = [(i, j) for i in range(len(left)) for j in range(len(right)) if i + j < count]
    left = [left[i] for i, _ in pairs]
    right = [right[j] for _, j in pairs]
    if len(pairs) > 1:
        left = jnp.concatenate(left, axis=0 if form == "tn" else 1)
        right = jnp.concatenate(right, axis=1 if form == "nt" else 0)
    else:
        left, right = left[0], right[0]
    return lax.dot_general(left, right, DIMS[form], preferred_element_type=F32)


def spread(x, group, wanted):
    x = jnp.where(group == wanted, x, 0.0)
    x = x + pltpu.roll(x, BASE, 1)
    return x + pltpu.roll(x, 2 * BASE, 1)


def pack_left(x, group):
    first = x.astype(BF16).astype(F32)
    rest = x - first
    second = rest.astype(BF16).astype(F32)
    third = rest - second
    one = jnp.where(group < 3, first, second)
    two = jnp.where(group == 0, second, jnp.where(group == 1, third, 0.0))
    return jnp.concatenate([one.astype(BF16), two.astype(BF16)], axis=1)


def pack_right(y):
    first, second, third = parts(y, 3)
    none = jnp.zeros(y.shape, BF16)
    return jnp.concatenate([first, second, third, first, second, first, none, none], axis=0)


def iota(shape, dim):
    return lax.broadcasted_iota(jnp.int32, shape, dim)


def take_block(ref, per_block, heads, head, block):
    rows = [ref[(block * per_block + r) * heads + head] for r in range(per_block)]
    return rows[0] if per_block == 1 else jnp.concatenate(rows, axis=0)


def put_block(ref, per_block, heads, head, block, value):
    size = value.shape[0] // per_block
    for r in range(per_block):
        ref[(block * per_block + r) * heads + head] = value[r * size : (r + 1) * size]


def eliminate(x, groups):
    tile = (groups, 8, 128)
    flat = (groups * 8, 128)
    lane = iota(tile, 2) % BASE
    row = iota(tile, 1)
    group_start = (iota(flat, 1) // BASE) * BASE
    x = x.reshape((groups, BASE, 128))
    tiles = [x[:, 8 * t : 8 * t + 8, :] for t in range(BASE // 8)]

    def pick(x, index):
        return jnp.take_along_axis(
            x.reshape(flat), index, axis=1, mode="promise_in_bounds"
        ).reshape(tile)

    for p in range(BASE - 1):
        home, at = p // 8, p % 8
        columns = {t: pick(tiles[t], group_start + p) for t in range(home, BASE // 8)}
        pivot = columns[home][:, at : at + 1, :]
        here = lane[:, :1] == p
        pivot_row = jnp.where(here, 1.0, tiles[home][:, at : at + 1, :])
        scaled = pivot_row * (1.0 / pivot)
        for t in range((p + 1) // 8, BASE // 8):
            new = jnp.where(lane == p, 0.0, tiles[t]) - columns[t] * scaled
            tiles[t] = jnp.where(row > at, new, tiles[t]) if t == home else new
    found = []
    for t in range(BASE // 8):
        pivots = pick(tiles[t], group_start + 8 * t + iota(flat, 0) % 8)
        position = row + 8 * t
        unit = jnp.where(lane < position, tiles[t], jnp.where(lane == position, 1.0, 0.0))
        found.append(unit * lax.rsqrt(pivots))
    return jnp.concatenate(found, axis=1).reshape(groups * BASE, 128)


def factor(a_ref, packed_ref, pairs, invert):
    groups = pairs // 4
    slab = (BASE, 128)
    square = (128, 128)

    def one_block(kb, carry):
        start = pl.multiple_of(kb * BASE, BASE)
        slab_group = iota(slab, 1) // BASE
        slabs = []
        for g in range(groups):
            joined = jnp.zeros(slab, F32)
            for h in range(4):
                rows = a_ref[4 * g + h, pl.ds(start, BASE), :]
                rows = pltpu.roll(rows, lax.rem((h - kb) * BASE + 128, 128), 1)
                joined = jnp.where(slab_group == h, rows, joined)
            slabs.append(joined)
        packed_ref[...] = eliminate(jnp.concatenate(slabs, axis=0), groups)

        def update(g, carry):
            packed = packed_ref[pl.ds(pl.multiple_of(g * BASE, BASE), BASE), :]
            turned = jnp.concatenate([packed, jnp.zeros((128 - BASE, 128), F32)], axis=0).T
            row_block = iota(square, 0) // BASE
            col_block = iota(square, 1) // BASE
            own = iota(slab, 1) == iota(slab, 0) + start
            for h in range(4):
                pair = 4 * g + h
                low = pack_left(spread(packed, slab_group, h), slab_group)
                low_t = pack_left(spread(turned[BASE * h : BASE * (h + 1)], slab_group, 0), slab_group)
                a = a_ref[pair]
                rows = a_ref[pair, pl.ds(start, BASE), :]
                rows = jnp.where(slab_group == kb, jnp.where(own, 1.0, 0.0), rows)
                top = mm(low, pack_right(rows))
                wide = mm(low_t, pack_right(top))
                gain = mm(pack_left(spread(a, col_block, kb), col_block), pack_right(wide))
                new = jnp.where(col_block == kb, 0.0, a) - gain
                if invert:
                    a_ref[pair] = new
                    a_ref[pair, pl.ds(start, BASE), :] = wide
                else:
                    a_ref[pair] = jnp.where(row_block > kb, new, a)
                    a_ref[pair, pl.ds(start, BASE), :] = jnp.where(slab_group <= kb, top, 0.0)
            return carry

        lax.fori_loop(0, groups, update, 0)
        return carry

    lax.fori_loop(0, 128 // BASE, one_block, 0)


def group_size(shards):
    size = 1
    while 4 * size * size <= shards and shards % (2 * size) == 0:
        size *= 2
    return size


def send(src, dst, send_sem, recv_sem, where):
    return pltpu.make_async_remote_copy(
        src_ref=src, dst_ref=dst, send_sem=send_sem, recv_sem=recv_sem,
        device_id=where, device_id_type=pl.DeviceIdType.MESH,
    )


def meet(head_parts, shards):
    size = group_size(shards)
    rank, me = lax.axis_index("seq"), lax.axis_index("head")
    outer, inner = rank // size, rank % size
    barrier = pltpu.get_barrier_semaphore()

    def greet(where):
        pl.semaphore_signal(barrier, inc=1, device_id=where, device_id_type=pl.DeviceIdType.MESH)

    for d in range(1, head_parts):
        greet((rank, lax.rem(me + d, head_parts)))
    for d in range(1, size):
        greet((outer * size + lax.rem(inner + d, size), me))

    @pl.when(outer > 0)
    def _():
        greet((rank - size, me))

    @pl.when(outer < shards // size - 1)
    def _():
        greet((rank + size, me))

    chained = jnp.where(outer > 0, 1, 0) + jnp.where(outer < shards // size - 1, 1, 0)
    pl.semaphore_wait(barrier, head_parts - 1 + size - 1 + chained)


class Scan:
    def __init__(self, shards, backward, own, near, before, total, sems):
        self.size = group_size(shards)
        self.count = shards // self.size
        self.rank, self.me = lax.axis_index("seq"), lax.axis_index("head")
        self.step = -self.size if backward else self.size
        self.base = self.rank // self.size * self.size
        self.inner = self.rank % self.size
        outer = self.rank // self.size
        self.outer = self.count - 1 - outer if backward else outer
        self.backward = backward
        self.own, self.near, self.before, self.total = own, near, before, total
        self.near_send, self.near_recv, self.far_send, self.far_recv = sems

    def near_copy(self, c, d):
        where = (self.base + lax.rem(self.inner + d, self.size), self.me)
        return send(
            self.own.at[c], self.near.at[d - 1, c],
            self.near_send.at[d - 1, c], self.near_recv.at[d - 1, c], where,
        )

    def far_copy(self, c):
        where = (self.rank + self.step, self.me)
        return send(self.total.at[c], self.before.at[c], self.far_send.at[c], self.far_recv.at[c], where)

    def start(self, c):
        for d in range(1, self.size):
            self.near_copy(c, d).start()

    def finish(self, c):
        whole = self.own[c]
        lower = jnp.zeros(whole.shape, F32)
        for d in range(1, self.size):
            self.near_copy(c, d).wait_recv()
            other = self.near[d - 1, c]
            whole = whole + other
            counts = d > self.inner if self.backward else d <= self.inner
            lower = lower + jnp.where(counts, other, 0.0)

        @pl.when(self.outer == 0)
        def _():
            self.before[c] = jnp.zeros(whole.shape, F32)

        @pl.when(self.outer > 0)
        def _():
            self.far_copy(c).wait_recv()

        before = self.before[c]

        @pl.when(self.outer < self.count - 1)
        def _():
            self.total[c] = before + whole
            self.far_copy(c).start()

        return before + lower

    def drain(self, c):
        for d in range(1, self.size):
            self.near_copy(c, d).wait_send()

        @pl.when(self.outer < self.count - 1)
        def _():
            self.far_copy(c).wait_send()


def scan_scratch(shards, heads, square):
    size = group_size(shards)
    count = 2 * heads
    near = (max(size - 1, 1), count)
    dma = pltpu.SemaphoreType.DMA
    return [
        pltpu.VMEM(near + square, F32), pltpu.VMEM((count,) + square, F32),
        pltpu.VMEM((count,) + square, F32), dma(near), dma(near), dma((count,)), dma((count,)),
    ]


def first_kernel(
    heads, blocks, per_block, head_parts, shards,
    q_in, k_in, v_in, g_in, q_ref, k_ref, v_ref, g_ref, before_ref,
    own, near, before, total, near_send, near_recv, far_send, far_recv,
    one_send, one_recv, all_send, all_recv,
):
    rank, me = lax.axis_index("seq"), lax.axis_index("head")
    meet(head_parts, shards)
    scan = Scan(shards, False, own, near, before, total, (near_send, near_recv, far_send, far_recv))

    def one_copy(i, d, h):
        src, dst = ((k_in, k_ref), (v_in, v_ref))[i]
        peer = lax.rem(me + d, head_parts)
        return send(
            src.at[peer * heads + h], dst.at[me * heads + h],
            one_send.at[i, d - 1, h], one_recv.at[i, d - 1, h], (rank, peer),
        )

    def all_copy(i, d):
        src, dst = ((q_in, q_ref), (g_in, g_ref))[i]
        peer = lax.rem(me + d, head_parts)
        return send(
            src.at[pl.ds(peer * heads, heads)], dst.at[pl.ds(me * heads, heads)],
            all_send.at[i, d - 1], all_recv.at[i, d - 1], (rank, peer),
        )

    steps = [(i, d, h) for h in range(heads) for i in range(2) for d in range(1, head_parts)]
    wholes = [(i, d) for i in range(2) for d in range(1, head_parts)]
    for step in steps:
        one_copy(*step).start()
    for step in wholes:
        all_copy(*step).start()
    for src, dst in ((k_in, k_ref), (v_in, v_ref), (q_in, q_ref), (g_in, g_ref)):
        for h in range(heads):
            dst[me * heads + h] = src[me * heads + h]
    for h in range(heads):
        for i in range(2):
            for d in range(1, head_parts):
                one_copy(i, d, h).wait_recv()
        gram = jnp.zeros((128, 128), F32)
        state = jnp.zeros((128, 128), F32)
        for block in range(blocks):
            k = take_block(k_ref, per_block, heads, h, block)
            v = take_block(v_ref, per_block, heads, h, block)
            gram += mm(k, k, "tn")
            state += mm(v, k, "tn")
        own[2 * h] = gram
        own[2 * h + 1] = state
        scan.start(2 * h)
        scan.start(2 * h + 1)
    for c in range(2 * heads):
        before_ref[c] = scan.finish(c)
    for step in wholes:
        all_copy(*step).wait_recv()
    for c in range(2 * heads):
        scan.drain(c)
    for step in steps:
        one_copy(*step).wait_send()
    for step in wholes:
        all_copy(*step).wait_send()


def main_kernel(
    heads, blocks, per_block,
    q_ref, k_ref, v_ref, g_ref, before_ref, regular_ref,
    o_ref, dq_ref, dk_ref, dv_ref, later_ref, sums_ref,
    p_ref, kp_ref, m_ref, state_ref, packed_ref,
):
    pairs = heads * blocks
    square = (128, 128)

    def prefix(head, carry):
        gram, state = before_ref[2 * head], before_ref[2 * head + 1]
        eye = iota(square, 0) == iota(square, 1)
        gram = gram + jnp.where(eye, regular_ref[pl.ds(head, 1), :], 0.0)
        for block in range(blocks):
            p_ref[head * blocks + block] = gram
            state_ref[head * blocks + block] = state
            if block + 1 < blocks:
                k = take_block(k_ref, per_block, heads, head, block)
                v = take_block(v_ref, per_block, heads, head, block)
                gram += mm(k, k, "tn")
                state += mm(v, k, "tn")
        return carry

    lax.fori_loop(0, heads, prefix, 0)
    factor(p_ref, packed_ref, pairs, True)

    def inner(head, carry):
        eye = (iota(square, 0) == iota(square, 1)).astype(F32)
        for block in range(blocks):
            pair = head * blocks + block
            k = take_block(k_ref, per_block, heads, head, block)
            kp = mm(k, p_ref[pair], "nn", 3)
            kp_ref[pair] = kp
            m_ref[pair] = eye + mm(kp, k, "nt", 3)
        return carry

    lax.fori_loop(0, heads, inner, 0)
    factor(m_ref, packed_ref, pairs, False)

    def outer(head, carry):
        upto = iota(square, 1) <= iota(square, 0)
        upto2 = iota((256, 128), 1) <= iota((256, 128), 0) % 128
        later_gram = jnp.zeros(square, F32)
        later_state = jnp.zeros(square, F32)
        for block in reversed(range(blocks)):
            pair = head * blocks + block
            q = take_block(q_ref, per_block, heads, head, block)
            k = take_block(k_ref, per_block, heads, head, block)
            v = take_block(v_ref, per_block, heads, head, block)
            g = take_block(g_ref, per_block, heads, head, block)
            kp = parts(kp_ref[pair], 3)
            m = parts(m_ref[pair], 3)
            state = parts(state_ref[pair], 2)
            both = [jnp.concatenate([p, r], axis=0) for p, r in zip(parts(p_ref[pair], 3), kp)]
            ct = jnp.where(upto, mm(g, v, "nt"), 0.0)
            rows = parts(mm(g, state, "nn") + mm(ct, k, "nn"), 3)
            none = jnp.zeros(square, BF16)
            rows = [jnp.concatenate([q if i == 0 else none, r], axis=0) for i, r in enumerate(rows)]
            firsts = mm(rows, both, "nt", 3)
            y = jnp.where(upto2, mm(firsts[:, 128:], m, "nt", 3), 0.0)
            x = jnp.where(upto2, mm(y, m, "nn", 3), 0.0)
            uz = firsts[:, :128] - mm(x, kp, "nn", 3)
            u, z = uz[:128], uz[128:]
            uzp = parts(uz, 2)
            up, zp = [t[:128] for t in uzp], [t[128:] for t in uzp]
            both_w = jnp.where(upto2, mm(uzp, k, "nt"), 0.0)
            wt = parts(both_w[:128], 2)
            w2t = both_w[128:]
            put_block(o_ref, per_block, heads, head, block, (mm(up, state, "nt") + mm(wt, v, "nn")).astype(BF16))
            put_block(dq_ref, per_block, heads, head, block, z.astype(BF16))
            dk_ref[pair] = mm(jnp.concatenate([ct - w2t, -both_w[:128]], axis=0), uzp, "tn")
            dv_ref[pair] = mm(wt, g, "tn")
            later_ref[pair] = later_gram
            later_ref[pairs + pair] = later_state
            zu = mm(zp, up, "tn")
            later_gram = later_gram - (zu + zu.T)
            later_state = later_state + mm(g, up, "tn")
        sums_ref[2 * head] = later_gram
        sums_ref[2 * head + 1] = later_state
        return carry

    lax.fori_loop(0, heads, outer, 0)


def last_kernel(
    heads, blocks, per_block, head_parts, shards,
    o_in, dq_in, k_ref, v_ref, dk_ref, dv_ref, later_ref, own, o_out, dq_out, dk_out, dv_out,
    dk_all, dv_all, near, after, total, near_send, near_recv, far_send, far_recv,
    one_send, one_recv, all_send, all_recv,
):
    pairs = heads * blocks
    rank, me = lax.axis_index("seq"), lax.axis_index("head")
    meet(head_parts, shards)
    scan = Scan(shards, True, own, near, after, total, (near_send, near_recv, far_send, far_recv))

    def one_copy(i, d, h):
        src, dst = ((dk_all, dk_out), (dv_all, dv_out))[i]
        peer = lax.rem(me + d, head_parts)
        return send(
            src.at[peer * heads + h], dst.at[me * heads + h],
            one_send.at[i, d - 1, h], one_recv.at[i, d - 1, h], (rank, peer),
        )

    def all_copy(i, d):
        src, dst = ((o_in, o_out), (dq_in, dq_out))[i]
        peer = lax.rem(me + d, head_parts)
        return send(
            src.at[pl.ds(peer * heads, heads)], dst.at[pl.ds(me * heads, heads)],
            all_send.at[i, d - 1], all_recv.at[i, d - 1], (rank, peer),
        )

    steps = [(i, d, h) for h in range(heads) for i in range(2) for d in range(1, head_parts)]
    wholes = [(i, d) for i in range(2) for d in range(1, head_parts)]
    for c in range(2 * heads):
        scan.start(c)
    for step in wholes:
        all_copy(*step).start()
    for src, dst in ((o_in, o_out), (dq_in, dq_out)):
        for h in range(heads):
            dst[me * heads + h] = src[me * heads + h]
    for h in range(heads):
        gram, state = scan.finish(2 * h), scan.finish(2 * h + 1)
        for block in range(blocks):
            pair = h * blocks + block
            k = take_block(k_ref, per_block, heads, h, block)
            v = take_block(v_ref, per_block, heads, h, block)
            sym = later_ref[pair] + gram
            state_after = parts(later_ref[pairs + pair] + state, 2)
            dk = dk_ref[pair] + mm(k, sym, "nn") + mm(v, state_after, "nn")
            dv = dv_ref[pair] + mm(k, state_after, "nt")
            put_block(dk_all, per_block, heads, h, block, dk.astype(BF16))
            put_block(dv_all, per_block, heads, h, block, dv.astype(BF16))
        for i in range(2):
            for d in range(1, head_parts):
                one_copy(i, d, h).start()
        dk_out[me * heads + h] = dk_all[me * heads + h]
        dv_out[me * heads + h] = dv_all[me * heads + h]
    for step in wholes:
        all_copy(*step).wait_recv()
    for step in steps:
        one_copy(*step).wait_recv()
    for c in range(2 * heads):
        scan.drain(c)
    for step in wholes:
        all_copy(*step).wait_send()
    for step in steps:
        one_copy(*step).wait_send()


def call(body, inputs, out_shape, scratch=(), flops=10**9, **params):
    vmem = pl.BlockSpec(memory_space=pltpu.VMEM)
    return pl.pallas_call(
        body,
        out_shape=out_shape,
        in_specs=[vmem] * len(inputs),
        out_specs=jax.tree.map(lambda _: vmem, out_shape),
        scratch_shapes=list(scratch),
        compiler_params=pltpu.CompilerParams(vmem_limit_bytes=VMEM_LIMIT, **params),
        cost_estimate=pl.CostEstimate(flops=flops, bytes_accessed=8 * 2**20, transcendentals=0),
    )(*inputs)


def on_device(head_parts, seq_parts, queries, keys, values, out_grad, regular):
    local = queries.shape[1]
    feature = queries.shape[2]
    heads = queries.shape[0] // head_parts
    blocks = head_parts * local // GROUP
    per_block = GROUP // local
    pairs = heads * blocks

    square = (feature, feature)

    def shape(count, kind=F32, rows=feature):
        return jax.ShapeDtypeStruct((count, rows, feature), kind)

    moved = jax.ShapeDtypeStruct(queries.shape, BF16)
    square_sums = shape(2 * heads)
    dma = pltpu.SemaphoreType.DMA
    away = max(head_parts - 1, 1)
    swap_sems = [dma((2, away, heads))] * 2 + [dma((2, away))] * 2
    sizes = (heads, blocks, per_block)
    queries, keys, values, out_grad, before = call(
        functools.partial(first_kernel, *sizes, head_parts, seq_parts),
        (queries, keys, values, out_grad),
        (moved,) * 4 + (square_sums,),
        [pltpu.VMEM((2 * heads,) + square, F32)] + scan_scratch(seq_parts, heads, square) + swap_sems,
        collective_id=0, has_side_effects=True,
    )
    output, dq, dk, dv, later, back = call(
        functools.partial(main_kernel, *sizes),
        (queries, keys, values, out_grad, before, regular),
        (moved, moved, shape(pairs), shape(pairs), shape(2 * pairs), square_sums),
        [pltpu.VMEM((pairs,) + square, F32)] * 4 + [pltpu.VMEM((pairs // 4 * BASE, 128), F32)],
    )
    return call(
        functools.partial(last_kernel, *sizes, head_parts, seq_parts),
        (output, dq, keys, values, dk, dv, later, back),
        (moved,) * 4,
        [pltpu.VMEM(moved.shape, BF16)] * 2 + scan_scratch(seq_parts, heads, square) + swap_sems,
        collective_id=1, has_side_effects=True,
    )


def solution(mesh):
    placed = P(None, ("seq", "head"), None)
    return jax.shard_map(
        functools.partial(on_device, mesh.shape["head"], mesh.shape["seq"]),
        mesh=mesh,
        in_specs=(placed,) * 4 + (P("head", None),),
        out_specs=(placed,) * 4,
        check_vma=False,
    )
```
